32 devices in a mesh: ctx: 4 (over x, core), row: 4 (over z), col: 2 (over y).
Axes of the slice: x: 2, y: 2, z: 4, core: 2. Of those that a mesh axis runs over, the one named last changes fastest.
Arguments:
- states: bfloat16 [384, 4096], P('ctx', 'row'), may hold values from -6 to 6
- context: bfloat16 [384, 4096], P('ctx', 'row'), may hold values from -6 to 6
- up_weight: bfloat16 [4096, 8192], P('row', 'col'), may hold values from -0.09375 to 0.09375
- down_weight: bfloat16 [8192, 4096], P('col', 'row'), may hold values from -0.0625 to 0.0625
- cotangent: bfloat16 [384, 4096], P('ctx', 'row'), may hold values from -6 to 6
Outputs:
- latent: bfloat16 [384, 4096], P('ctx', 'row')
- logdet: float32 [384], P(('ctx', 'row'))
- grad_states: bfloat16 [384, 4096], P('ctx', 'row')
- grad_context: bfloat16 [384, 4096], P('ctx', 'row')
- grad_up: float32 [4096, 8192], P('row', 'col')
- grad_down: float32 [8192, 4096], P('col', 'row')
The draws below stay inside these ranges and needn't reach their ends.
All inputs are finite; a program needn't handle non-finite values.
Results may differ from the reference program's by a relative error of at most 0.024.
Values may be sent and summed in bfloat16 or wider, within the bound.
A program may use at most 192 MiB of HBM per device.

```python
import jax
import jax.numpy as jnp
from jax import lax

D = 4096
HF = 8192
TOK_CTX = 96
TOKENS = 384
N_CTX = 4
N_ROW = 4
N_COL = 2


def raised(values, key, source, target, shards_of, factor):
    owner, partner = [(jnp.arange(values.shape[axis_at]) // (values.shape[axis_at] // shards_of)).reshape([-1 if axis == axis_at else 1 for axis in range(values.ndim)]) for axis_at in (source, target)]
    chosen = jax.random.permutation(key, shards_of)[partner]
    strong = (owner == chosen) | (owner == (partner + shards_of // 2) % shards_of)
    return jnp.where(strong, factor * values, values)


def steps_of(key, extent, split, smallest, largest):
    factor_of = 1.0
    for dim, parts in split:
        draws = jax.random.uniform(jax.random.fold_in(jax.random.fold_in(key, 6), dim), (parts,), jnp.float32, smallest / len(split), largest / len(split))
        factor_of = factor_of * jnp.repeat(jnp.exp(draws), extent[dim] // parts).reshape((-1,) + (1,) * (len(extent) - 1 - dim))
    return factor_of


def centred(own_key, shape, deviation, most, split=(), dtype=jnp.bfloat16):
    factor_of = steps_of(own_key, shape, split, -0.22, 0.18) if split else 1.0
    values = jax.random.normal(own_key, shape, jnp.float32) * deviation * factor_of
    return jnp.minimum(jnp.maximum(values, -most), most).astype(dtype)


def bell_draw_with(key, dims, deviation, limit, cuts, heavy, held_as=jnp.bfloat16):
    values = deviation * jax.random.normal(key, dims, jnp.float32)
    if cuts:
        values = values * steps_of(key, dims, cuts, -0.22, 0.18)
    return jnp.clip(raised(values, jax.random.fold_in(key, 3), *heavy), -limit, limit).astype(held_as)


def setup_inputs(seed: int = 0) -> dict:
    streams_of = jax.random.split(jax.random.key(seed), 6)
    return {
        "states": centred(streams_of[0], (TOKENS, D), 1.0, 6.0, ((0, 4), (1, 4))),
        "context": bell_draw_with(streams_of[1], (TOKENS, D), 1.0, 6.0, ((0, 4), (1, 4)), (1, 0, 4, 2.0)),
        "up_weight": centred(streams_of[2], (D, HF), D ** -0.5, 0.09375, ((0, 4), (1, 2))),
        "down_weight": centred(streams_of[3], (HF, D), HF ** -0.5, 0.0625, ((0, 2), (1, 4))),
        "cotangent": centred(streams_of[4], (TOKENS, D), 1.0, 6.0, ((0, 4), (1, 4))),
    }


def to_half(values):
    rounded = values.astype(jnp.bfloat16)
    rounded = lax.optimization_barrier(rounded)
    return rounded.astype(jnp.float32)


def silu_slope(hidden):
    sigmoid_part = jax.nn.sigmoid(hidden)
    return sigmoid_part * (1.0 + hidden * (1.0 - sigmoid_part))


def reference(states, context, up_weight, down_weight, cotangent):
    feat_width = D // N_ROW
    unit_width = HF // N_COL
    hidden = jnp.zeros((TOKENS, HF), jnp.float32)
    for index in range(N_ROW):
        lower = index * feat_width
        upper = lower + feat_width
        product = jnp.dot(context[:, lower:upper], up_weight[lower:upper, :], preferred_element_type=jnp.float32)
        hidden = hidden + to_half(product)
    acts = jax.nn.silu(hidden).astype(jnp.bfloat16)
    mixed = jnp.zeros((TOKENS, D), jnp.float32)
    for index in range(N_COL):
        lower = index * unit_width
        upper = lower + unit_width
        product = jnp.dot(acts[:, lower:upper], down_weight[lower:upper, :], preferred_element_type=jnp.float32)
        mixed = mixed + to_half(product)
    log_scale = jnp.tanh(mixed)
    shrink = jnp.exp(-log_scale)
    flowed = states.astype(jnp.float32) * shrink
    latent = flowed.astype(jnp.bfloat16)
    logdet = -jnp.sum(log_scale, axis=1)
    scale_grad = ((1.0 - cotangent.astype(jnp.float32) * flowed) * (1.0 - log_scale * log_scale)).astype(jnp.bfloat16)
    back = jnp.zeros((TOKENS, HF), jnp.float32)
    for index in range(N_ROW):
        lower = index * feat_width
        upper = lower + feat_width
        product = jnp.dot(scale_grad[:, lower:upper], down_weight[:, lower:upper].T, preferred_element_type=jnp.float32)
        back = back + to_half(product)
    slope = (back * silu_slope(hidden)).astype(jnp.bfloat16)
    input_total = jnp.zeros((TOKENS, D), jnp.float32)
    for index in range(N_COL):
        lower = index * unit_width
        upper = lower + unit_width
        product = jnp.dot(slope[:, lower:upper], up_weight[:, lower:upper].T, preferred_element_type=jnp.float32)
        input_total = input_total + to_half(product)
    grad_states = (cotangent.astype(jnp.float32) * shrink).astype(jnp.bfloat16)
    grad_context = input_total.astype(jnp.bfloat16)
    grad_up = jnp.zeros((D, HF), jnp.float32)
    grad_down = jnp.zeros((HF, D), jnp.float32)
    for index in range(N_CTX):
        lower = index * TOK_CTX
        upper = lower + TOK_CTX
        up_part = jnp.dot(context[lower:upper, :].T, slope[lower:upper, :], preferred_element_type=jnp.float32)
        down_part = jnp.dot(acts[lower:upper, :].T, scale_grad[lower:upper, :], preferred_element_type=jnp.float32)
        grad_up = grad_up + to_half(up_part)
        grad_down = grad_down + to_half(down_part)
    return latent, logdet, grad_states, grad_context, grad_up, grad_down
```

```python
import jax
import jax.numpy as jnp
from jax import lax
from jax.sharding import PartitionSpec as P


def silu_slope(hidden):
    sigmoid_part = jax.nn.sigmoid(hidden)
    return sigmoid_part * (1.0 + hidden * (1.0 - sigmoid_part))


def collect(row_block):
    return lax.all_gather(row_block, "row", axis=0, tiled=True)


def every_patch(group_rows):
    return lax.all_gather(group_rows, "ctx", axis=0, tiled=True)


def feature_total(partial_terms):
    return lax.psum(partial_terms.astype(jnp.bfloat16), "col").astype(jnp.float32)


def contract(left_side, right_side, left_dim, right_dim):
    return lax.dot_general(
        left_side,
        right_side,
        (((left_dim,), (right_dim,)), ((), ())),
        preferred_element_type=jnp.float32,
    )


def shards(states, context, up_weight, down_weight, cotangent):
    hidden = lax.psum_scatter(
        jnp.dot(context, up_weight, preferred_element_type=jnp.float32).astype(jnp.bfloat16),
        "row",
        scatter_dimension=0,
        tiled=True,
    ).astype(jnp.float32)
    activations = collect(jax.nn.silu(hidden).astype(jnp.bfloat16))
    output_terms = jnp.dot(activations, down_weight, preferred_element_type=jnp.float32)
    mixed_total = feature_total(output_terms)
    log_scale = jnp.tanh(mixed_total)
    shrink = jnp.exp(-log_scale)
    flowed = states.astype(jnp.float32) * shrink
    cotangent_wide = cotangent.astype(jnp.float32)
    det_terms = -jnp.sum(log_scale, axis=1)
    scale_rows = ((1.0 - cotangent_wide * flowed) * (1.0 - log_scale * log_scale)).astype(
        jnp.bfloat16
    )
    grad_down = contract(every_patch(activations), every_patch(scale_rows), 0, 0)
    back_terms = contract(scale_rows, down_weight, 1, 1)
    back_rows = lax.psum_scatter(
        back_terms.astype(jnp.bfloat16), "row", scatter_dimension=0, tiled=True
    ).astype(jnp.float32)
    logdet = lax.psum_scatter(det_terms, "row", scatter_dimension=0, tiled=True)
    slope_rows = (back_rows * silu_slope(hidden)).astype(jnp.bfloat16)
    slope_all = collect(slope_rows)
    input_terms = contract(slope_all, up_weight, 1, 1)
    grad_states = (cotangent_wide * shrink).astype(jnp.bfloat16)
    grad_context = feature_total(input_terms).astype(jnp.bfloat16)
    grad_up = contract(every_patch(context), every_patch(slope_all), 0, 0)
    return (flowed.astype(jnp.bfloat16), logdet, grad_states, grad_context, grad_up, grad_down)


def solution(mesh):
    placed = (P("ctx", "row"), P("ctx", "row"), P("row", "col"), P("col", "row"), P("ctx", "row"))
    return jax.shard_map(
        shards,
        mesh=mesh,
        in_specs=placed,
        out_specs=(
            P("ctx", "row"),
            P(("ctx", "row")),
            P("ctx", "row"),
            P("ctx", "row"),
            P("row", "col"),
            P("col", "row"),
        ),
        check_vma=False,
    )
```

```python
import functools

import jax
import jax.numpy as jnp
from jax import lax
from jax.experimental import pallas as pl
from jax.experimental.pallas import tpu as pltpu
from jax.sharding import PartitionSpec as P


def silu_slope(hidden):
    sigmoid_part = jax.nn.sigmoid(hidden)
    return sigmoid_part * (1.0 + hidden * (1.0 - sigmoid_part))


def collect(row_block):
    return lax.all_gather(row_block, "row", axis=0, tiled=True)


def every_patch(group_rows, ways):
    blocks = [group_rows]
    bit = ways // 2
    while bit:
        pairs = [(i, i ^ bit) for i in range(ways)]
        blocks = blocks + [lax.ppermute(block, "ctx", pairs) for block in blocks]
        bit //= 2
    return blocks


def feature_total(partial_terms, ways):
    sent = partial_terms.astype(jnp.bfloat16)
    if ways != 2:
        return lax.psum(sent, "col").astype(jnp.float32)
    other = lax.ppermute(sent, "col", [(0, 1), (1, 0)])
    return sent.astype(jnp.float32) + other.astype(jnp.float32)


def row_pieces(values, ways):
    me = lax.axis_index("row")
    rows = values.shape[0] // ways
    total = None
    for shift in range(1, ways):
        piece = lax.dynamic_slice_in_dim(values, (me + shift) % ways * rows, rows)
        came = lax.ppermute(piece, "row", [(i, (i + shift) % ways) for i in range(ways)])
        total = came.astype(jnp.float32) if total is None else total + came.astype(jnp.float32)
    return total + lax.dynamic_slice_in_dim(values, me * rows, rows).astype(jnp.float32)


def row_scatter(partial_terms, ways):
    sent = partial_terms.astype(jnp.bfloat16)
    if ways == 4:
        return row_pieces(sent, ways)
    return lax.psum_scatter(sent, "row", scatter_dimension=0, tiled=True).astype(jnp.float32)


def contract(left_side, right_side, left_dim, right_dim):
    return lax.dot_general(
        left_side,
        right_side,
        (((left_dim,), (right_dim,)), ((), ())),
        preferred_element_type=jnp.float32,
    )


def outer_kernel(count, *refs):
    lefts, rights, out_ref = refs[:count], refs[count : 2 * count], refs[2 * count]
    left = jnp.concatenate([ref[...] for ref in lefts], axis=0)
    right = jnp.concatenate([ref[...] for ref in rights], axis=0)
    out_ref[...] = contract(left, right, 0, 0)


def outer_total(lefts, rights):
    count = len(lefts)
    patches, height = lefts[0].shape
    width = rights[0].shape[1]
    tall = height >= width
    tile = min(512, max(height, width))
    if tall:
        left_spec = pl.BlockSpec((patches, tile), lambda i: (0, i))
        right_spec = pl.BlockSpec((patches, width), lambda i: (0, 0))
        out_spec = pl.BlockSpec((tile, width), lambda i: (i, 0))
    else:
        left_spec = pl.BlockSpec((patches, height), lambda i: (0, 0))
        right_spec = pl.BlockSpec((patches, tile), lambda i: (0, i))
        out_spec = pl.BlockSpec((height, tile), lambda i: (0, i))
    return pl.pallas_call(
        functools.partial(outer_kernel, count),
        grid=(max(height, width) // tile,),
        in_specs=[left_spec] * count + [right_spec] * count,
        out_specs=out_spec,
        out_shape=jax.ShapeDtypeStruct((height, width), jnp.float32),
        compiler_params=pltpu.CompilerParams(vmem_limit_bytes=40 * 1024 * 1024),
        cost_estimate=pl.CostEstimate(
            flops=2 * count * patches * height * width,
            bytes_accessed=4 * height * width + 2 * count * patches * (height + width),
            transcendentals=0,
        ),
    )(*lefts, *rights)


def shards(n_ctx, n_row, n_col, states, context, up_weight, down_weight, cotangent):
    hidden = row_scatter(jnp.dot(context, up_weight, preferred_element_type=jnp.float32), n_row)
    context_blocks = every_patch(context, n_ctx)
    activations = collect(jax.nn.silu(hidden).astype(jnp.bfloat16))
    acts_blocks = every_patch(activations, n_ctx)
    output_terms = jnp.dot(activations, down_weight, preferred_element_type=jnp.float32)
    log_scale = jnp.tanh(feature_total(output_terms, n_col))
    shrink = jnp.exp(-log_scale)
    flowed = states.astype(jnp.float32) * shrink
    cotangent_wide = cotangent.astype(jnp.float32)
    det_terms = -jnp.sum(log_scale, axis=1)
    scale_rows = ((1.0 - cotangent_wide * flowed) * (1.0 - log_scale * log_scale)).astype(
        jnp.bfloat16
    )
    back_terms = contract(scale_rows, down_weight, 1, 1)
    back_rows = row_scatter(back_terms, n_row)
    scale_blocks = every_patch(scale_rows, n_ctx)
    grad_down = outer_total(acts_blocks, scale_blocks)
    if n_row == 4:
        logdet = row_pieces(det_terms, n_row)
    else:
        logdet = lax.psum_scatter(det_terms, "row", scatter_dimension=0, tiled=True)
    slope_rows = (back_rows * silu_slope(hidden)).astype(jnp.bfloat16)
    slope_all = collect(slope_rows)
    slope_blocks = every_patch(slope_all, n_ctx)
    input_terms = contract(slope_all, up_weight, 1, 1)
    grad_states = (cotangent_wide * shrink).astype(jnp.bfloat16)
    grad_context = feature_total(input_terms, n_col).astype(jnp.bfloat16)
    grad_up = outer_total(context_blocks, slope_blocks)
    return (flowed.astype(jnp.bfloat16), logdet, grad_states, grad_context, grad_up, grad_down)


def solution(mesh):
    placed = (P("ctx", "row"), P("ctx", "row"), P("row", "col"), P("col", "row"), P("ctx", "row"))
    return jax.shard_map(
        functools.partial(shards, mesh.shape["ctx"], mesh.shape["row"], mesh.shape["col"]),
        mesh=mesh,
        in_specs=placed,
        out_specs=(
            P("ctx", "row"),
            P(("ctx", "row")),
            P("ctx", "row"),
            P("ctx", "row"),
            P("row", "col"),
            P("col", "row"),
        ),
        check_vma=False,
    )
```

```python
import functools

import jax
import jax.numpy as jnp
from jax import lax
from jax.experimental import pallas as pl
from jax.experimental.pallas import tpu as pltpu
from jax.sharding import PartitionSpec as P


def silu_slope(hidden):
    sigmoid_part = jax.nn.sigmoid(hidden)
    return sigmoid_part * (1.0 + hidden * (1.0 - sigmoid_part))


def collect(row_block):
    return lax.all_gather(row_block, "row", axis=0, tiled=True)


def every_patch(group_rows, ways):
    return finish_patches(first_patch(group_rows, ways), ways)


def first_patch(group_rows, ways):
    far = ways // 2
    return [group_rows, lax.ppermute(group_rows, "ctx", [(i, i ^ far) for i in range(ways)])]


def finish_patches(blocks, ways):
    bit = ways // 4
    while bit:
        pairs = [(i, i ^ bit) for i in range(ways)]
        blocks = blocks + [lax.ppermute(block, "ctx", pairs) for block in blocks]
        bit //= 2
    return blocks


def feature_total(partial_terms, ways):
    sent = partial_terms.astype(jnp.bfloat16)
    if ways != 2:
        return lax.psum(sent, "col").astype(jnp.float32)
    other = lax.ppermute(sent, "col", [(0, 1), (1, 0)])
    return sent.astype(jnp.float32) + other.astype(jnp.float32)


def row_pieces(values, ways):
    me = lax.axis_index("row")
    rows = values.shape[0] // ways
    total = None
    for shift in range(1, ways):
        piece = lax.dynamic_slice_in_dim(values, (me + shift) % ways * rows, rows)
        came = lax.ppermute(piece, "row", [(i, (i + shift) % ways) for i in range(ways)])
        total = came.astype(jnp.float32) if total is None else total + came.astype(jnp.float32)
    return total + lax.dynamic_slice_in_dim(values, me * rows, rows).astype(jnp.float32)


def row_scatter(partial_terms, ways):
    sent = partial_terms.astype(jnp.bfloat16)
    if ways == 4:
        return row_pieces(sent, ways)
    return lax.psum_scatter(sent, "row", scatter_dimension=0, tiled=True).astype(jnp.float32)


def contract(left_side, right_side, left_dim, right_dim):
    return lax.dot_general(
        left_side,
        right_side,
        (((left_dim,), (right_dim,)), ((), ())),
        preferred_element_type=jnp.float32,
    )


def outer_kernel(count, *refs):
    lefts, rights, out_ref = refs[:count], refs[count : 2 * count], refs[2 * count]
    left = jnp.concatenate([ref[...] for ref in lefts], axis=0)
    right = jnp.concatenate([ref[...] for ref in rights], axis=0)
    out_ref[...] = contract(left, right, 0, 0)


def outer_total(lefts, rights):
    count = len(lefts)
    patches, height = lefts[0].shape
    width = rights[0].shape[1]
    tall = height >= width
    tile = min(512, max(height, width))
    if tall:
        left_spec = pl.BlockSpec((patches, tile), lambda i: (0, i))
        right_spec = pl.BlockSpec((patches, width), lambda i: (0, 0))
        out_spec = pl.BlockSpec((tile, width), lambda i: (i, 0))
    else:
        left_spec = pl.BlockSpec((patches, height), lambda i: (0, 0))
        right_spec = pl.BlockSpec((patches, tile), lambda i: (0, i))
        out_spec = pl.BlockSpec((height, tile), lambda i: (0, i))
    return pl.pallas_call(
        functools.partial(outer_kernel, count),
        grid=(max(height, width) // tile,),
        in_specs=[left_spec] * count + [right_spec] * count,
        out_specs=out_spec,
        out_shape=jax.ShapeDtypeStruct((height, width), jnp.float32),
        compiler_params=pltpu.CompilerParams(vmem_limit_bytes=40 * 1024 * 1024),
        cost_estimate=pl.CostEstimate(
            flops=2 * count * patches * height * width,
            bytes_accessed=4 * height * width + 2 * count * patches * (height + width),
            transcendentals=0,
        ),
    )(*lefts, *rights)


def shards(n_ctx, n_row, n_col, states, context, up_weight, down_weight, cotangent):
    hidden = row_scatter(jnp.dot(context, up_weight, preferred_element_type=jnp.float32), n_row)
    context_far = first_patch(context, n_ctx)
    activations = collect(jax.nn.silu(hidden).astype(jnp.bfloat16))
    acts_far = first_patch(activations, n_ctx)
    output_terms = jnp.dot(activations, down_weight, preferred_element_type=jnp.float32)
    log_scale = jnp.tanh(feature_total(output_terms, n_col))
    shrink = jnp.exp(-log_scale)
    flowed = states.astype(jnp.float32) * shrink
    cotangent_wide = cotangent.astype(jnp.float32)
    det_terms = -jnp.sum(log_scale, axis=1)
    scale_rows = ((1.0 - cotangent_wide * flowed) * (1.0 - log_scale * log_scale)).astype(
        jnp.bfloat16
    )
    scale_rows, acts_far, context_far = lax.optimization_barrier((scale_rows, acts_far, context_far))
    back_terms = contract(scale_rows, down_weight, 1, 1)
    back_rows = row_scatter(back_terms, n_row)
    scale_far = first_patch(scale_rows, n_ctx)
    slope_rows = (back_rows * silu_slope(hidden)).astype(jnp.bfloat16)
    slope_rows, acts_far, scale_far, context_far = lax.optimization_barrier(
        (slope_rows, acts_far, scale_far, context_far)
    )
    slope_all = collect(slope_rows)
    slope_all, acts_far, scale_far, context_far, det_terms = lax.optimization_barrier(
        (slope_all, acts_far, scale_far, context_far, det_terms)
    )
    slope_far = first_patch(slope_all, n_ctx)
    input_terms = contract(slope_all, up_weight, 1, 1).astype(jnp.bfloat16)
    acts_blocks = finish_patches(acts_far, n_ctx)
    scale_blocks = finish_patches(scale_far, n_ctx)
    context_blocks = finish_patches(context_far, n_ctx)
    if n_row == 4:
        logdet = row_pieces(det_terms, n_row)
    else:
        logdet = lax.psum_scatter(det_terms, "row", scatter_dimension=0, tiled=True)
    grad_states = (cotangent_wide * shrink).astype(jnp.bfloat16)
    grad_down = outer_total(acts_blocks, scale_blocks)
    slope_far, grad_down, context_blocks, input_terms = lax.optimization_barrier(
        (slope_far, grad_down, context_blocks, input_terms)
    )
    slope_blocks = finish_patches(slope_far, n_ctx)
    grad_context = feature_total(input_terms, n_col).astype(jnp.bfloat16)
    grad_up = outer_total(context_blocks, slope_blocks)
    return (flowed.astype(jnp.bfloat16), logdet, grad_states, grad_context, grad_up, grad_down)


def solution(mesh):
    placed = (P("ctx", "row"), P("ctx", "row"), P("row", "col"), P("col", "row"), P("ctx", "row"))
    return jax.shard_map(
        functools.partial(shards, mesh.shape["ctx"], mesh.shape["row"], mesh.shape["col"]),
        mesh=mesh,
        in_specs=placed,
        out_specs=(
            P("ctx", "row"),
            P(("ctx", "row")),
            P("ctx", "row"),
            P("ctx", "row"),
            P("row", "col"),
            P("col", "row"),
        ),
        check_vma=False,
    )
```

```python
import functools

import jax
import jax.numpy as jnp
from jax import lax
from jax.experimental import pallas as pl
from jax.experimental.pallas import tpu as pltpu
from jax.sharding import PartitionSpec as P


def silu_slope(hidden):
    sigmoid_part = jax.nn.sigmoid(hidden)
    return sigmoid_part * (1.0 + hidden * (1.0 - sigmoid_part))


def collect(row_block):
    return lax.all_gather(row_block, "row", axis=0, tiled=True)


def every_patch(group_rows, ways):
    return finish_patches(first_patch(group_rows, ways), ways)


def first_patch(group_rows, ways):
    far = ways // 2
    return [group_rows, lax.ppermute(group_rows, "ctx", [(i, i ^ far) for i in range(ways)])]


def finish_patches(blocks, ways):
    bit = ways // 4
    while bit:
        pairs = [(i, i ^ bit) for i in range(ways)]
        blocks = blocks + [lax.ppermute(block, "ctx", pairs) for block in blocks]
        bit //= 2
    return blocks


def feature_total(partial_terms, ways):
    sent = partial_terms.astype(jnp.bfloat16)
    if ways != 2:
        return lax.psum(sent, "col").astype(jnp.float32)
    other = lax.ppermute(sent, "col", [(0, 1), (1, 0)])
    return sent.astype(jnp.float32) + other.astype(jnp.float32)


def row_pieces(values, ways):
    me = lax.axis_index("row")
    rows = values.shape[0] // ways
    total = None
    for shift in range(1, ways):
        piece = lax.dynamic_slice_in_dim(values, (me + shift) % ways * rows, rows)
        came = lax.ppermute(piece, "row", [(i, (i + shift) % ways) for i in range(ways)])
        total = came.astype(jnp.float32) if total is None else total + came.astype(jnp.float32)
    return total + lax.dynamic_slice_in_dim(values, me * rows, rows).astype(jnp.float32)


def row_scatter(partial_terms, ways):
    sent = partial_terms.astype(jnp.bfloat16)
    if ways == 4:
        return row_pieces(sent, ways)
    return lax.psum_scatter(sent, "row", scatter_dimension=0, tiled=True).astype(jnp.float32)


def contract(left_side, right_side, left_dim, right_dim):
    return lax.dot_general(
        left_side,
        right_side,
        (((left_dim,), (right_dim,)), ((), ())),
        preferred_element_type=jnp.float32,
    )


def outer_kernel(count, *refs):
    lefts, rights, out_ref = refs[:count], refs[count : 2 * count], refs[2 * count]
    left = jnp.concatenate([ref[...] for ref in lefts], axis=0)
    right = jnp.concatenate([ref[...] for ref in rights], axis=0)
    out_ref[...] = contract(left, right, 0, 0)


def outer_total(lefts, rights):
    count = len(lefts)
    patches, height = lefts[0].shape
    width = rights[0].shape[1]
    tall = height >= width
    tile = min(512, max(height, width))
    if tall:
        left_spec = pl.BlockSpec((patches, tile), lambda i: (0, i))
        right_spec = pl.BlockSpec((patches, width), lambda i: (0, 0))
        out_spec = pl.BlockSpec((tile, width), lambda i: (i, 0))
    else:
        left_spec = pl.BlockSpec((patches, height), lambda i: (0, 0))
        right_spec = pl.BlockSpec((patches, tile), lambda i: (0, i))
        out_spec = pl.BlockSpec((height, tile), lambda i: (0, i))
    return pl.pallas_call(
        functools.partial(outer_kernel, count),
        grid=(max(height, width) // tile,),
        in_specs=[left_spec] * count + [right_spec] * count,
        out_specs=out_spec,
        out_shape=jax.ShapeDtypeStruct((height, width), jnp.float32),
        compiler_params=pltpu.CompilerParams(vmem_limit_bytes=40 * 1024 * 1024),
        cost_estimate=pl.CostEstimate(
            flops=2 * count * patches * height * width,
            bytes_accessed=4 * height * width + 2 * count * patches * (height + width),
            transcendentals=0,
        ),
    )(*lefts, *rights)


def shards(n_ctx, n_row, n_col, states, context, up_weight, down_weight, cotangent):
    hidden = row_scatter(jnp.dot(context, up_weight, preferred_element_type=jnp.float32), n_row)
    context_far = first_patch(context, n_ctx)
    activations = collect(jax.nn.silu(hidden).astype(jnp.bfloat16))
    acts_far = first_patch(activations, n_ctx)
    output_terms = jnp.dot(activations, down_weight, preferred_element_type=jnp.float32)
    log_scale = jnp.tanh(feature_total(output_terms, n_col))
    shrink = jnp.exp(-log_scale)
    flowed = states.astype(jnp.float32) * shrink
    cotangent_wide = cotangent.astype(jnp.float32)
    det_terms = -jnp.sum(log_scale, axis=1)
    scale_rows = ((1.0 - cotangent_wide * flowed) * (1.0 - log_scale * log_scale)).astype(
        jnp.bfloat16
    )
    scale_rows, acts_far, context_far = lax.optimization_barrier((scale_rows, acts_far, context_far))
    back_terms = contract(scale_rows, down_weight, 1, 1)
    back_rows = row_scatter(back_terms, n_row)
    scale_far = first_patch(scale_rows, n_ctx)
    slope_rows = (back_rows * silu_slope(hidden)).astype(jnp.bfloat16)
    slope_rows, acts_far, scale_far, context_far = lax.optimization_barrier(
        (slope_rows, acts_far, scale_far, context_far)
    )
    slope_all = collect(slope_rows)
    slope_all, acts_far, scale_far, context_far, det_terms = lax.optimization_barrier(
        (slope_all, acts_far, scale_far, context_far, det_terms)
    )
    slope_far = first_patch(slope_all, n_ctx)
    input_terms = contract(slope_all, up_weight, 1, 1).astype(jnp.bfloat16)
    acts_blocks = finish_patches(acts_far, n_ctx)
    scale_blocks = finish_patches(scale_far, n_ctx)
    context_blocks = finish_patches(context_far, n_ctx)
    if n_row == 4:
        logdet = row_pieces(det_terms, n_row)
    else:
        logdet = lax.psum_scatter(det_terms, "row", scatter_dimension=0, tiled=True)
    grad_states = (cotangent_wide * shrink).astype(jnp.bfloat16)
    grad_down = outer_total(acts_blocks, scale_blocks)
    grad_context = feature_total(input_terms, n_col).astype(jnp.bfloat16)
    slope_far, grad_down, context_blocks, grad_context, logdet = lax.optimization_barrier(
        (slope_far, grad_down, context_blocks, grad_context, logdet)
    )
    slope_blocks = finish_patches(slope_far, n_ctx)
    grad_up = outer_total(context_blocks, slope_blocks)
    return (flowed.astype(jnp.bfloat16), logdet, grad_states, grad_context, grad_up, grad_down)


def solution(mesh):
    placed = (P("ctx", "row"), P("ctx", "row"), P("row", "col"), P("col", "row"), P("ctx", "row"))
    return jax.shard_map(
        functools.partial(shards, mesh.shape["ctx"], mesh.shape["row"], mesh.shape["col"]),
        mesh=mesh,
        in_specs=placed,
        out_specs=(
            P("ctx", "row"),
            P(("ctx", "row")),
            P("ctx", "row"),
            P("ctx", "row"),
            P("row", "col"),
            P("col", "row"),
        ),
        check_vma=False,
    )
```
